32 devices in a mesh: rep: 8 (over z, y), fsdp: 4 (over x, core).
Axes of the slice: x: 2, y: 2, z: 4, core: 2. Of those that a mesh axis runs over, the one named last changes fastest.
Arguments:
- tokens: bfloat16 [16384, 4096], P(('rep', 'fsdp')), may hold values from -6 to 6
- gate_pre: bfloat16 [16384, 768], P(('rep', 'fsdp')), may hold values from -8 to 8
- upstream: bfloat16 [16384, 768], P(('rep', 'fsdp')), may hold values from -6 to 6
- slow: float32 [8, 4096, 768], P('rep', 'fsdp'), may hold values from -6 to 6
- inner_mom: bfloat16 [8, 4096, 768], P('rep', 'fsdp'), may hold values from -6 to 6
- outer_mom: bfloat16 [8, 4096, 768], P('rep', 'fsdp'), may hold values from -3 to 3
- pairing: int32 [8], replicated, may hold values from 0 to 7, as said below
Outputs:
- gate_grad: bfloat16 [16384, 768], P(('rep', 'fsdp'))
- inner_new: bfloat16 [8, 4096, 768], P('rep', 'fsdp')
- outer_new: bfloat16 [8, 4096, 768], P('rep', 'fsdp')
- slow_new: float32 [8, 4096, 768], P('rep', 'fsdp')
The draws below stay inside these ranges and needn't reach their ends.
Inputs may be any that keep to these rules, and one draw needn't show every extreme that they name: pairing[i] = i XOR p for one p of 1 to 7 shared by all i, so pairing[pairing[i]] = i.
All inputs are finite; a program needn't handle non-finite values.
Results may differ from the reference program's by a relative error of at most 0.009.
Values may be sent and summed in bfloat16 or wider, within the bound.
A program may use at most 128 MiB of HBM per device.

```python
import jax
import jax.numpy as jnp
from jax import lax

D = 4096
COLS = 768
GROUP_ROWS = 2048
TOKENS = 16384
N_REP = 8


def draw_pairing(key, part):
    partner_xor = jax.random.randint(jax.random.fold_in(key, 17), (), 1, N_REP, dtype=jnp.int32)
    return jnp.bitwise_xor(jnp.arange(N_REP, dtype=jnp.int32), partner_xor)


def block_scale(stream_key, extent, cuts, smallest, largest):
    factor_of = 1.0
    for position, shards_of in cuts:
        draws = jax.random.uniform(jax.random.fold_in(jax.random.fold_in(stream_key, 6), position), (shards_of,), jnp.float32, smallest / len(cuts), largest / len(cuts))
        factor_of = factor_of * jnp.repeat(jnp.exp(draws), extent[position] // shards_of).reshape((-1,) + (1,) * (len(extent) - 1 - position))
    return factor_of


def gaussian(key, extent, width, bound, split=(), kind=jnp.bfloat16):
    result = jax.random.normal(key, extent, jnp.float32) * width
    if len(split) > 0:
        result = block_scale(key, extent, split, -0.22, 0.18) * result
    return jnp.clip(result, min=-bound, max=bound).astype(kind)


def setup_inputs(seed: int = 0) -> dict:
    key_of = jax.random.split(jax.random.key(seed), 8)
    tokens = gaussian(key_of[0], (TOKENS, D), 1.0, 6.0, ((0, 32),))
    gate_pre = gaussian(key_of[1], (TOKENS, COLS), 1.5, 8.0, ((0, 32),))
    upstream = gaussian(key_of[2], (TOKENS, COLS), 1.0, 6.0, ((0, 32),))
    slow = gaussian(key_of[3], (N_REP, D, COLS), 1.0, 6.0, ((0, 8), (1, 4)), jnp.float32)
    inner_mom = gaussian(key_of[4], (N_REP, D, COLS), 1.0, 6.0, ((0, 8), (1, 4)))
    outer_mom = gaussian(key_of[5], (N_REP, D, COLS), 0.5, 3.0, ((0, 8), (1, 4)))
    pairing = draw_pairing(jax.random.fold_in(key_of[7], 71), 0)
    return {"tokens": tokens, "gate_pre": gate_pre, "upstream": upstream, "slow": slow, "inner_mom": inner_mom, "outer_mom": outer_mom, "pairing": pairing}


inner_beta = 0.9
inner_rate = 0.5
outer_mu = 0.9
outer_rate = 0.7


def reference(tokens, gate_pre, upstream, slow, inner_mom, outer_mom, pairing):
    weight_scale = float(D) ** -0.5
    token_blocks = tokens.reshape(N_REP, GROUP_ROWS, D)
    gate_blocks = gate_pre.reshape(N_REP, GROUP_ROWS, COLS)
    upstream_blocks = upstream.reshape(N_REP, GROUP_ROWS, COLS)
    fast_weight = slow.astype(jnp.bfloat16)

    def replica_pass(blocks):
        token_rows, gate_rows, upstream_rows, fast_block = blocks
        up_values = jnp.dot(token_rows, fast_block, preferred_element_type=jnp.float32) * weight_scale
        gate_values = gate_rows.astype(jnp.float32)
        sigmoid_gate = jax.nn.sigmoid(gate_values)
        upstream_values = upstream_rows.astype(jnp.float32)
        grad_rows = (upstream_values * gate_values * sigmoid_gate).astype(jnp.bfloat16)
        gate_grad = (upstream_values * up_values * sigmoid_gate * (1.0 + gate_values * (1.0 - sigmoid_gate))).astype(jnp.bfloat16)
        weight_grad = jnp.dot(token_rows.T, grad_rows, preferred_element_type=jnp.float32) * weight_scale
        return gate_grad, weight_grad

    gate_grad, weight_grad = lax.map(replica_pass, (token_blocks, gate_blocks, upstream_blocks, fast_weight))
    inner_new = (inner_beta * inner_mom.astype(jnp.float32) + weight_grad).astype(jnp.bfloat16)
    outer_grad = slow - (fast_weight.astype(jnp.float32) - inner_rate * inner_new.astype(jnp.float32))
    mean_slow = 0.5 * (slow + slow[pairing])
    mean_grad = 0.5 * (outer_grad + outer_grad[pairing])
    outer_new = (outer_mu * outer_mom.astype(jnp.float32) + mean_grad).astype(jnp.bfloat16)
    slow_new = mean_slow - outer_rate * (mean_grad + outer_mu * outer_new.astype(jnp.float32))
    return gate_grad.reshape(TOKENS, COLS), inner_new, outer_new, slow_new
```

```python
import functools

import jax
import jax.numpy as jnp
from jax import lax
from jax.experimental import pallas as pl
from jax.experimental.pallas import tpu as pltpu
from jax.sharding import PartitionSpec as P

inner_beta = 0.9
inner_rate = 0.5
outer_mu = 0.9
outer_rate = 0.7

MESH = pl.DeviceIdType.MESH
F32 = jnp.float32
BF16 = jnp.bfloat16
CHUNK = 256
STRIP = 16


def flipped(index, mask):
    out = index
    for bit in range(mask.bit_length()):
        if mask >> bit & 1:
            out = out + (1 - 2 * lax.rem(lax.div(index, 1 << bit), 2)) * (1 << bit)
    return out


def kernel(
    xor, n, far, scale,
    tok, gate, ups, slow, imom, omom,
    gate_grad, inner_new, outer_new, slow_new,
    fast, grad, s1_out, s1_in, s2_out, s2_in, own, og_out, og_in, slow_in, acc,
    slow_sem, s1_sem, s2_sem, ag_sem, fw_sem, og_sem,
):
    rows = slow.shape[0]
    piece = min(CHUNK, rows)
    count = rows // piece
    chips = n // 2
    rep, me = lax.axis_index("rep"), lax.axis_index("fsdp")
    chip, core = lax.div(me, 2), lax.rem(me, 2)
    sibling = (rep, chip * 2 + 1 - core)
    partner = (flipped(rep, xor), me)

    def ahead(j):
        return lax.rem(chip + j, chips)

    def behind(j):
        return lax.rem(chip + chips - j, chips)

    def part(k):
        return pl.ds(pl.multiple_of(k * piece, piece), piece)

    def weight_part(block, k):
        start = pl.multiple_of(block * rows + k * piece, piece)
        return lax.dot_general(
            tok[:, pl.ds(start, piece)], grad[...], (((0,), (0,)), ((), ())),
            preferred_element_type=F32,
        )

    def remote(src, dst, sems, slot, device):
        return pltpu.make_async_remote_copy(
            src_ref=src, dst_ref=dst, send_sem=sems.at[0, slot], recv_sem=sems.at[1, slot],
            device_id=device, device_id_type=MESH,
        )

    def s1_copy(j, k):
        return remote(s1_out.at[j, part(k)], s1_in.at[j, part(k)], s1_sem, j * count + k, sibling)

    def s2_copy(j, k):
        return remote(
            s2_out.at[j - 1, part(k)], s2_in.at[j - 1, part(k)], s2_sem, (j - 1) * count + k,
            (rep, ahead(j) * 2 + core),
        )

    def ag_copy(j, k, block):
        return remote(
            fast.at[block, part(k)], fast.at[block, part(k)], ag_sem, (j - 1) * count + k,
            (rep, ahead(j) * 2 + core),
        )

    def fw_copy(j, k, block):
        return remote(
            fast.at[block, part(k)], fast.at[block, part(k)], fw_sem, j * count + k, sibling
        )

    def og_copy(k):
        return remote(og_out.at[part(k)], og_in.at[part(k)], og_sem, k, partner)

    def loop(stop, body, start=0):
        def step(i, carry):
            body(i)
            return carry

        lax.fori_loop(start, stop, step, 0)

    barrier = pltpu.get_barrier_semaphore()
    pl.semaphore_signal(barrier, inc=1, device_id=sibling, device_id_type=MESH)
    pl.semaphore_signal(barrier, inc=1, device_id=partner, device_id_type=MESH)
    for j in range(1, chips):
        pl.semaphore_signal(
            barrier, inc=1, device_id=(rep, ahead(j) * 2 + core), device_id_type=MESH
        )

    def cast_slow(i):
        at = pl.ds(pl.multiple_of(i * STRIP, STRIP), STRIP)
        fast[me, at, :] = slow[at, :].astype(BF16)

    loop(rows // STRIP, cast_slow)

    pl.semaphore_wait(barrier, chips + 1)
    slow_copy = remote(fast.at[me], slow_in, slow_sem, 0, partner)
    slow_copy.start()

    def make_grad(i):
        at = pl.ds(pl.multiple_of(i * STRIP, STRIP), STRIP)
        g = gate[at, :].astype(F32)
        grad[at, :] = (ups[at, :].astype(F32) * g * jax.nn.sigmoid(g)).astype(BF16)

    loop(grad.shape[0] // STRIP, make_grad)

    def first_hop(j, k):
        block = ahead(j) * 2 + 1 - core
        s1_out[j, part(k), :] = weight_part(block, k).astype(BF16)
        s1_copy(j, k).start()

    def second_hop(j, k):
        mine = weight_part(ahead(j) * 2 + core, k)
        s1_copy(j, k).wait_recv()
        s2_out[j - 1, part(k), :] = (mine + s1_in[j, part(k), :].astype(F32)).astype(BF16)
        s2_copy(j, k).start()

    remote_parts = (chips - 1) * count
    loop(remote_parts, lambda t: first_hop(lax.div(t, count) + 1, lax.rem(t, count)))
    loop(remote_parts, lambda t: second_hop(lax.div(t, count) + 1, lax.rem(t, count)))
    loop(count, lambda k: first_hop(0, k))
    loop(count, lambda k: fw_copy(0, k, me).start())

    def own_part(k):
        own[part(k), :] = weight_part(me, k)

    loop(count, own_part)

    def own_sum(k):
        s1_copy(0, k).wait_recv()
        for j in range(1, chips):
            s2_copy(j, k).wait_recv()

        def strip(i):
            at = pl.ds(pl.multiple_of(k * piece + i * STRIP, STRIP), STRIP)
            total = own[at, :] + s1_in[0, at, :].astype(F32)
            for j in range(1, chips):
                total = total + s2_in[j - 1, at, :].astype(F32)
            new = (inner_beta * imom[at, :].astype(F32) + total * scale).astype(BF16)
            inner_new[at, :] = new
            og = slow[at, :] - (fast[me, at, :].astype(F32) - inner_rate * new.astype(F32))
            own[at, :] = og
            og_out[at, :] = og.astype(BF16)

        loop(piece // STRIP, strip)
        og_copy(k).start()

    def gather_part(k):
        for j in range(1, chips):
            ag_copy(j, k, me).start()

    def up_part(block, k, first):
        start = pl.multiple_of(block * rows + k * piece, piece)
        value = jnp.dot(
            tok[:, pl.ds(start, piece)], fast[block, part(k), :], preferred_element_type=F32
        )
        acc[...] = value if first else acc[...] + value

    up_part(me, 0, True)
    loop(count, lambda k: up_part(me, k, False), start=1)

    loop(count - 1, own_sum)
    gather_part(0)
    own_sum(count - 1)
    loop(count, gather_part, start=1)

    def sibling_part(k):
        fw_copy(0, k, me).wait_recv()
        up_part(chip * 2 + 1 - core, k, False)

    loop(count, sibling_part)

    def finish_weights():
        slow_copy.wait_recv()

        def finish(k):
            og_copy(k).wait_recv()

            def strip(i):
                at = pl.ds(pl.multiple_of(k * piece + i * STRIP, STRIP), STRIP)
                mean_slow = 0.5 * (slow[at, :] + slow_in[at, :].astype(F32))
                mean_grad = 0.5 * (own[at, :] + og_in[at, :].astype(F32))
                new = (outer_mu * omom[at, :].astype(F32) + mean_grad).astype(BF16)
                outer_new[at, :] = new
                slow_new[at, :] = mean_slow - outer_rate * (
                    mean_grad + outer_mu * new.astype(F32)
                )

            loop(piece // STRIP, strip)

        loop(count, finish)

    def finish_gate():
        def gathered(t):
            j, k = lax.div(t, count) + 1, lax.rem(t, count)
            block = behind(j) * 2 + core
            ag_copy(j, k, block).wait_recv()
            fw_copy(j, k, block).start()
            up_part(block, k, False)
            fw_copy(j, k, block).wait_recv()
            up_part(behind(j) * 2 + 1 - core, k, False)

        loop(remote_parts, gathered)

        def strip(i):
            at = pl.ds(pl.multiple_of(i * STRIP, STRIP), STRIP)
            g = gate[at, :].astype(F32)
            s = jax.nn.sigmoid(g)
            gate_grad[at, :] = (
                ups[at, :].astype(F32) * (acc[at, :] * scale) * s * (1.0 + g * (1.0 - s))
            ).astype(BF16)

        loop(acc.shape[0] // STRIP, strip)

    if far:
        finish_gate()
        finish_weights()
    else:
        finish_weights()
        finish_gate()

    slow_copy.wait_send()

    def drain(k):
        og_copy(k).wait_send()
        for j in range(chips):
            s1_copy(j, k).wait_send()
            fw_copy(j, k, behind(j) * 2 + core).wait_send()
        for j in range(1, chips):
            s2_copy(j, k).wait_send()
            ag_copy(j, k, me).wait_send()

    loop(count, drain)


def outer_step(xor, n_rep, n, scale, tokens, gate_pre, upstream, slow, inner_mom, outer_mom):
    rows, cols = slow.shape
    held = tokens.shape[0]
    chips = n // 2
    count = rows // min(CHUNK, rows)
    vmem = pl.BlockSpec(memory_space=pltpu.VMEM)
    flops = 4 * held * tokens.shape[1] * cols
    return pl.pallas_call(
        functools.partial(kernel, xor, n, 2 * xor >= n_rep, scale),
        out_shape=(
            jax.ShapeDtypeStruct((held, cols), BF16),
            jax.ShapeDtypeStruct((rows, cols), BF16),
            jax.ShapeDtypeStruct((rows, cols), BF16),
            jax.ShapeDtypeStruct((rows, cols), F32),
        ),
        in_specs=[vmem] * 6,
        out_specs=(vmem,) * 4,
        scratch_shapes=[
            pltpu.VMEM((n, rows, cols), BF16),
            pltpu.VMEM((held, cols), BF16),
            pltpu.VMEM((chips, rows, cols), BF16),
            pltpu.VMEM((chips, rows, cols), BF16),
            pltpu.VMEM((chips - 1, rows, cols), BF16),
            pltpu.VMEM((chips - 1, rows, cols), BF16),
            pltpu.VMEM((rows, cols), F32),
            pltpu.VMEM((rows, cols), BF16),
            pltpu.VMEM((rows, cols), BF16),
            pltpu.VMEM((rows, cols), BF16),
            pltpu.VMEM((held, cols), F32),
            pltpu.SemaphoreType.DMA((2, 1)),
            pltpu.SemaphoreType.DMA((2, chips * count)),
            pltpu.SemaphoreType.DMA((2, (chips - 1) * count)),
            pltpu.SemaphoreType.DMA((2, (chips - 1) * count)),
            pltpu.SemaphoreType.DMA((2, chips * count)),
            pltpu.SemaphoreType.DMA((2, count)),
        ],
        compiler_params=pltpu.CompilerParams(
            collective_id=xor, has_side_effects=True, vmem_limit_bytes=56 * 1024 * 1024
        ),
        cost_estimate=pl.CostEstimate(
            flops=flops, bytes_accessed=2 * tokens.size + 22 * slow.size, transcendentals=0
        ),
    )(tokens, gate_pre, upstream, slow, inner_mom, outer_mom)


def solution(mesh):
    n_rep, n = mesh.shape["rep"], mesh.shape["fsdp"]

    def local(tokens, gate_pre, upstream, slow, inner_mom, outer_mom, pairing):
        scale = float(tokens.shape[1]) ** -0.5
        branches = [
            functools.partial(outer_step, xor, n_rep, n, scale) for xor in range(1, n_rep)
        ]
        gate_grad, inner_new, outer_new, slow_new = lax.switch(
            pairing[0] - 1, branches,
            tokens, gate_pre, upstream, slow[0], inner_mom[0], outer_mom[0],
        )
        return gate_grad, inner_new[None], outer_new[None], slow_new[None]

    rows, weights = P(("rep", "fsdp"), None), P("rep", "fsdp", None)
    return jax.shard_map(
        local,
        mesh=mesh,
        in_specs=(rows, rows, rows, weights, weights, weights, P()),
        out_specs=(rows, weights, weights, weights),
        check_vma=False,
    )
```

```python
import functools

import jax
import jax.numpy as jnp
from jax import lax
from jax.experimental import pallas as pl
from jax.experimental.pallas import tpu as pltpu
from jax.sharding import PartitionSpec as P

inner_beta = 0.9
inner_rate = 0.5
outer_mu = 0.9
outer_rate = 0.7

MESH = pl.DeviceIdType.MESH
F32 = jnp.float32
BF16 = jnp.bfloat16
CHUNK = 256
STRIP = 16
GATE_PIECES = 4


def flipped(index, mask):
    out = index
    for bit in range(mask.bit_length()):
        if mask >> bit & 1:
            out = out + (1 - 2 * lax.rem(lax.div(index, 1 << bit), 2)) * (1 << bit)
    return out


def kernel(
    xor, n, far, scale,
    tok_hbm, gate_hbm, ups_hbm, slow_hbm, imom_hbm, omom_hbm,
    gate_grad_hbm, inner_new_hbm, outer_new_hbm, slow_new_hbm,
    tok, gate, ups, slow, imom, omom, gate_grad, inner_new, outer_new, slow_new,
    fast, grad, s1_out, s1_in, s2_out, s2_in, own, og_out, og_in, slow_in, acc,
    in_sem, out_sem, slow_sem, s1_sem, s2_sem, ag_sem, fw_sem, og_sem,
):
    rows = slow.shape[0]
    piece = min(CHUNK, rows)
    count = rows // piece
    early = count // 2
    chips = n // 2
    rep, me = lax.axis_index("rep"), lax.axis_index("fsdp")
    chip, core = lax.div(me, 2), lax.rem(me, 2)
    sibling = (rep, chip * 2 + 1 - core)
    partner = (flipped(rep, xor), me)

    def ahead(j):
        return lax.rem(chip + j, chips)

    def behind(j):
        return lax.rem(chip + chips - j, chips)

    def part(k):
        return pl.ds(pl.multiple_of(k * piece, piece), piece)

    def weight_part(block, k):
        start = pl.multiple_of(block * rows + k * piece, piece)
        return lax.dot_general(
            tok[:, pl.ds(start, piece)], grad[...], (((0,), (0,)), ((), ())),
            preferred_element_type=F32,
        )

    def remote(src, dst, sems, slot, device):
        return pltpu.make_async_remote_copy(
            src_ref=src, dst_ref=dst, send_sem=sems.at[0, slot], recv_sem=sems.at[1, slot],
            device_id=device, device_id_type=MESH,
        )

    def s1_copy(j, k):
        return remote(s1_out.at[j, part(k)], s1_in.at[j, part(k)], s1_sem, j * count + k, sibling)

    def s2_copy(j, k):
        return remote(
            s2_out.at[j - 1, part(k)], s2_in.at[j - 1, part(k)], s2_sem, (j - 1) * count + k,
            (rep, ahead(j) * 2 + core),
        )

    def ag_copy(j, k, block):
        return remote(
            fast.at[block, part(k)], fast.at[block, part(k)], ag_sem, (j - 1) * count + k,
            (rep, ahead(j) * 2 + core),
        )

    def fw_copy(j, k, block):
        return remote(
            fast.at[block, part(k)], fast.at[block, part(k)], fw_sem, j * count + k, sibling
        )

    def og_copy(k):
        return remote(og_out.at[part(k)], og_in.at[part(k)], og_sem, k, partner)

    def loop(stop, body, start=0):
        def step(i, carry):
            body(i)
            return carry

        lax.fori_loop(start, stop, step, 0)

    def slow_load(k):
        return pltpu.make_async_copy(slow_hbm.at[part(k)], slow.at[part(k)], in_sem.at[5 + k])

    def load(i):
        src, dst = ((gate_hbm, gate), (ups_hbm, ups), (tok_hbm, tok), (imom_hbm, imom), (omom_hbm, omom))[i]
        return pltpu.make_async_copy(src, dst, in_sem.at[i])

    def store(i, k):
        src, dst = ((inner_new, inner_new_hbm), (outer_new, outer_new_hbm), (slow_new, slow_new_hbm))[i]
        return pltpu.make_async_copy(src.at[part(k)], dst.at[part(k)], out_sem.at[i * count + k])

    tall = gate_grad.shape[0] // GATE_PIECES

    def gate_store(k):
        at = pl.ds(pl.multiple_of(k * tall, tall), tall)
        return pltpu.make_async_copy(
            gate_grad.at[at], gate_grad_hbm.at[at], out_sem.at[3 * count + k]
        )

    barrier = pltpu.get_barrier_semaphore()
    pl.semaphore_signal(barrier, inc=1, device_id=sibling, device_id_type=MESH)
    pl.semaphore_signal(barrier, inc=1, device_id=partner, device_id_type=MESH)
    for j in range(1, chips):
        pl.semaphore_signal(
            barrier, inc=1, device_id=(rep, ahead(j) * 2 + core), device_id_type=MESH
        )

    loop(count, lambda k: slow_load(k).start())
    for i in range(5):
        load(i).start()

    def cast_slow(k):
        slow_load(k).wait()

        def strip(i):
            at = pl.ds(pl.multiple_of(k * piece + i * STRIP, STRIP), STRIP)
            fast[me, at, :] = slow[at, :].astype(BF16)

        loop(piece // STRIP, strip)

    def slow_copy(k):
        return remote(fast.at[me, part(k)], slow_in.at[part(k)], slow_sem, k, partner)

    def gather_part(k):
        for j in range(1, chips):
            ag_copy(j, k, me).start()

    cast_slow(0)
    pl.semaphore_wait(barrier, chips + 1)

    def send_slow(k):
        slow_copy(k).start()

    send_slow(0)

    def cast_and_send(k):
        cast_slow(k)
        send_slow(k)

    loop(count, cast_and_send, start=1)
    loop(early, gather_part)
    load(0).wait()
    load(1).wait()

    def make_grad(i):
        at = pl.ds(pl.multiple_of(i * STRIP, STRIP), STRIP)
        g = gate[at, :].astype(F32)
        grad[at, :] = (ups[at, :].astype(F32) * g * jax.nn.sigmoid(g)).astype(BF16)

    loop(grad.shape[0] // STRIP, make_grad)

    load(2).wait()

    def first_hop(j, k):
        block = ahead(j) * 2 + 1 - core
        s1_out[j, part(k), :] = weight_part(block, k).astype(BF16)
        s1_copy(j, k).start()

    def second_hop(j, k):
        mine = weight_part(ahead(j) * 2 + core, k)
        s1_copy(j, k).wait_recv()
        s2_out[j - 1, part(k), :] = (mine + s1_in[j, part(k), :].astype(F32)).astype(BF16)
        s2_copy(j, k).start()

    remote_parts = (chips - 1) * count
    loop(remote_parts, lambda t: first_hop(lax.div(t, count) + 1, lax.rem(t, count)))
    loop(remote_parts, lambda t: second_hop(lax.div(t, count) + 1, lax.rem(t, count)))
    loop(count, lambda k: first_hop(0, k))
    loop(count, lambda k: fw_copy(0, k, me).start())

    def own_part(k):
        own[part(k), :] = weight_part(me, k)

    loop(count, own_part)

    def own_sum(k):
        s1_copy(0, k).wait_recv()
        for j in range(1, chips):
            s2_copy(j, k).wait_recv()

        def strip(i):
            at = pl.ds(pl.multiple_of(k * piece + i * STRIP, STRIP), STRIP)
            total = own[at, :] + s1_in[0, at, :].astype(F32)
            for j in range(1, chips):
                total = total + s2_in[j - 1, at, :].astype(F32)
            new = (inner_beta * imom[at, :].astype(F32) + total * scale).astype(BF16)
            inner_new[at, :] = new
            og = slow[at, :] - (fast[me, at, :].astype(F32) - inner_rate * new.astype(F32))
            own[at, :] = og
            og_out[at, :] = og.astype(BF16)

        loop(piece // STRIP, strip)
        og_copy(k).start()
        store(0, k).start()

    def up_part(block, k, first):
        start = pl.multiple_of(block * rows + k * piece, piece)
        value = jnp.dot(
            tok[:, pl.ds(start, piece)], fast[block, part(k), :], preferred_element_type=F32
        )
        acc[...] = value if first else acc[...] + value

    up_part(me, 0, True)
    loop(count, lambda k: up_part(me, k, False), start=1)

    def sibling_part(k):
        fw_copy(0, k, me).wait_recv()
        up_part(chip * 2 + 1 - core, k, False)

    loop(count, sibling_part)

    def gathered(j, k):
        block = behind(j) * 2 + core
        ag_copy(j, k, block).wait_recv()
        fw_copy(j, k, block).start()
        up_part(block, k, False)
        fw_copy(j, k, block).wait_recv()
        up_part(behind(j) * 2 + 1 - core, k, False)

    for j in range(1, chips):
        loop(early, functools.partial(gathered, j))
    load(3).wait()
    loop(count - 1, own_sum)
    loop(min(early + 1, count), gather_part, start=early)
    own_sum(count - 1)
    loop(count, gather_part, start=early + 1)

    def finish_weights():
        load(4).wait()

        def finish(k):
            slow_copy(k).wait_recv()
            og_copy(k).wait_recv()

            def strip(i):
                at = pl.ds(pl.multiple_of(k * piece + i * STRIP, STRIP), STRIP)
                mean_slow = 0.5 * (slow[at, :] + slow_in[at, :].astype(F32))
                mean_grad = 0.5 * (own[at, :] + og_in[at, :].astype(F32))
                new = (outer_mu * omom[at, :].astype(F32) + mean_grad).astype(BF16)
                outer_new[at, :] = new
                slow_new[at, :] = mean_slow - outer_rate * (
                    mean_grad + outer_mu * new.astype(F32)
                )

            loop(piece // STRIP, strip)
            store(1, k).start()
            store(2, k).start()

        loop(count, finish)

    def finish_gate():
        for j in range(1, chips):
            loop(count, functools.partial(gathered, j), start=early)

        def gate_piece(k):
            def strip(i):
                at = pl.ds(pl.multiple_of(k * tall + i * STRIP, STRIP), STRIP)
                g = gate[at, :].astype(F32)
                s = jax.nn.sigmoid(g)
                gate_grad[at, :] = (
                    ups[at, :].astype(F32) * (acc[at, :] * scale) * s * (1.0 + g * (1.0 - s))
                ).astype(BF16)

            loop(tall // STRIP, strip)
            gate_store(k).start()

        loop(GATE_PIECES, gate_piece)

    if far:
        finish_gate()
        finish_weights()
    else:
        finish_weights()
        finish_gate()

    def drain(k):
        slow_copy(k).wait_send()
        og_copy(k).wait_send()
        for j in range(chips):
            s1_copy(j, k).wait_send()
            fw_copy(j, k, behind(j) * 2 + core).wait_send()
        for j in range(1, chips):
            s2_copy(j, k).wait_send()
            ag_copy(j, k, me).wait_send()
        for i in range(3):
            store(i, k).wait()

    loop(count, drain)
    loop(GATE_PIECES, lambda k: gate_store(k).wait())


def outer_step(xor, n_rep, n, scale, tokens, gate_pre, upstream, slow, inner_mom, outer_mom):
    rows, cols = slow.shape
    held = tokens.shape[0]
    chips = n // 2
    count = rows // min(CHUNK, rows)
    hbm = pl.BlockSpec(memory_space=pl.ANY)
    flops = 4 * held * tokens.shape[1] * cols
    return pl.pallas_call(
        functools.partial(kernel, xor, n, 2 * xor >= n_rep, scale),
        out_shape=(
            jax.ShapeDtypeStruct((held, cols), BF16),
            jax.ShapeDtypeStruct((rows, cols), BF16),
            jax.ShapeDtypeStruct((rows, cols), BF16),
            jax.ShapeDtypeStruct((rows, cols), F32),
        ),
        in_specs=[hbm] * 6,
        out_specs=(hbm,) * 4,
        scratch_shapes=[
            pltpu.VMEM(tokens.shape, BF16),
            pltpu.VMEM((held, cols), BF16),
            pltpu.VMEM((held, cols), BF16),
            pltpu.VMEM((rows, cols), F32),
            pltpu.VMEM((rows, cols), BF16),
            pltpu.VMEM((rows, cols), BF16),
            pltpu.VMEM((held, cols), BF16),
            pltpu.VMEM((rows, cols), BF16),
            pltpu.VMEM((rows, cols), BF16),
            pltpu.VMEM((rows, cols), F32),
            pltpu.VMEM((n, rows, cols), BF16),
            pltpu.VMEM((held, cols), BF16),
            pltpu.VMEM((chips, rows, cols), BF16),
            pltpu.VMEM((chips, rows, cols), BF16),
            pltpu.VMEM((chips - 1, rows, cols), BF16),
            pltpu.VMEM((chips - 1, rows, cols), BF16),
            pltpu.VMEM((rows, cols), F32),
            pltpu.VMEM((rows, cols), BF16),
            pltpu.VMEM((rows, cols), BF16),
            pltpu.VMEM((rows, cols), BF16),
            pltpu.VMEM((held, cols), F32),
            pltpu.SemaphoreType.DMA((5 + count,)),
            pltpu.SemaphoreType.DMA((3 * count + GATE_PIECES,)),
            pltpu.SemaphoreType.DMA((2, count)),
            pltpu.SemaphoreType.DMA((2, chips * count)),
            pltpu.SemaphoreType.DMA((2, (chips - 1) * count)),
            pltpu.SemaphoreType.DMA((2, (chips - 1) * count)),
            pltpu.SemaphoreType.DMA((2, chips * count)),
            pltpu.SemaphoreType.DMA((2, count)),
        ],
        compiler_params=pltpu.CompilerParams(
            collective_id=xor, has_side_effects=True, vmem_limit_bytes=56 * 1024 * 1024
        ),
        cost_estimate=pl.CostEstimate(
            flops=flops, bytes_accessed=2 * tokens.size + 22 * slow.size, transcendentals=0
        ),
    )(tokens, gate_pre, upstream, slow, inner_mom, outer_mom)


def solution(mesh):
    n_rep, n = mesh.shape["rep"], mesh.shape["fsdp"]

    def local(tokens, gate_pre, upstream, slow, inner_mom, outer_mom, pairing):
        scale = float(tokens.shape[1]) ** -0.5
        branches = [
            functools.partial(outer_step, xor, n_rep, n, scale) for xor in range(1, n_rep)
        ]
        gate_grad, inner_new, outer_new, slow_new = lax.switch(
            pairing[0] - 1, branches,
            tokens, gate_pre, upstream, slow[0], inner_mom[0], outer_mom[0],
        )
        return gate_grad, inner_new[None], outer_new[None], slow_new[None]

    rows, weights = P(("rep", "fsdp"), None), P("rep", "fsdp", None)
    return jax.shard_map(
        local,
        mesh=mesh,
        in_specs=(rows, rows, rows, weights, weights, weights, P()),
        out_specs=(rows, weights, weights, weights),
        check_vma=False,
    )
```

```python
import functools

import jax
import jax.numpy as jnp
from jax import lax
from jax.experimental import pallas as pl
from jax.experimental.pallas import tpu as pltpu
from jax.sharding import PartitionSpec as P

inner_beta = 0.9
inner_rate = 0.5
outer_mu = 0.9
outer_rate = 0.7

MESH = pl.DeviceIdType.MESH
F32 = jnp.float32
BF16 = jnp.bfloat16
CHUNK = 256
STRIP = 16
GATE_PIECES = 4


def flipped(index, mask):
    out = index
    for bit in range(mask.bit_length()):
        if mask >> bit & 1:
            out = out + (1 - 2 * lax.rem(lax.div(index, 1 << bit), 2)) * (1 << bit)
    return out


def kernel(
    xor, n, far, scale,
    tok_hbm, gate_hbm, ups_hbm, slow_hbm, imom_hbm, omom_hbm,
    gate_grad, inner_new, outer_new, slow_new,
    tok, gate, ups, slow, imom, omom,
    fast, grad, s1_out, s1_in, s2_out, s2_in, own, og_out, og_in, slow_in, acc, factor,
    in_sem, slow_sem, s1_sem, s2_sem, ag_sem, fw_sem, og_sem,
):
    rows = slow.shape[0]
    piece = min(CHUNK, rows)
    count = rows // piece
    early = count // 2
    chips = n // 2
    rep, me = lax.axis_index("rep"), lax.axis_index("fsdp")
    chip, core = lax.div(me, 2), lax.rem(me, 2)
    sibling = (rep, chip * 2 + 1 - core)
    partner = (flipped(rep, xor), me)

    def ahead(j):
        return lax.rem(chip + j, chips)

    def behind(j):
        return lax.rem(chip + chips - j, chips)

    def part(k):
        return pl.ds(pl.multiple_of(k * piece, piece), piece)

    def weight_part(block, k):
        start = pl.multiple_of(block * rows + k * piece, piece)
        return lax.dot_general(
            tok[:, pl.ds(start, piece)], grad[...], (((0,), (0,)), ((), ())),
            preferred_element_type=F32,
        )

    def remote(src, dst, sems, slot, device):
        return pltpu.make_async_remote_copy(
            src_ref=src, dst_ref=dst, send_sem=sems.at[0, slot], recv_sem=sems.at[1, slot],
            device_id=device, device_id_type=MESH,
        )

    def s1_copy(j, k):
        return remote(s1_out.at[j, part(k)], s1_in.at[j, part(k)], s1_sem, j * count + k, sibling)

    def s2_copy(j, k):
        return remote(
            s2_out.at[j - 1, part(k)], s2_in.at[j - 1, part(k)], s2_sem, (j - 1) * count + k,
            (rep, ahead(j) * 2 + core),
        )

    def ag_copy(j, k, block):
        return remote(
            fast.at[block, part(k)], fast.at[block, part(k)], ag_sem, (j - 1) * count + k,
            (rep, ahead(j) * 2 + core),
        )

    def fw_copy(j, k, block):
        return remote(
            fast.at[block, part(k)], fast.at[block, part(k)], fw_sem, j * count + k, sibling
        )

    def og_copy(k):
        return remote(og_out.at[part(k)], og_in.at[part(k)], og_sem, k, partner)

    def loop(stop, body, start=0):
        def step(i, carry):
            body(i)
            return carry

        lax.fori_loop(start, stop, step, 0)

    def slow_load(k):
        return pltpu.make_async_copy(slow_hbm.at[part(k)], slow.at[part(k)], in_sem.at[5 + k])

    def load(i):
        src, dst = ((gate_hbm, gate), (ups_hbm, ups), (tok_hbm, tok), (imom_hbm, imom), (omom_hbm, omom))[i]
        return pltpu.make_async_copy(src, dst, in_sem.at[i])

    tall = gate_grad.shape[0] // GATE_PIECES

    barrier = pltpu.get_barrier_semaphore()
    pl.semaphore_signal(barrier, inc=1, device_id=sibling, device_id_type=MESH)
    pl.semaphore_signal(barrier, inc=1, device_id=partner, device_id_type=MESH)
    for j in range(1, chips):
        pl.semaphore_signal(
            barrier, inc=1, device_id=(rep, ahead(j) * 2 + core), device_id_type=MESH
        )

    loop(count, lambda k: slow_load(k).start())
    for i in range(5):
        load(i).start()

    def cast_slow(k):
        slow_load(k).wait()

        def strip(i):
            at = pl.ds(pl.multiple_of(k * piece + i * STRIP, STRIP), STRIP)
            fast[me, at, :] = slow[at, :].astype(BF16)

        loop(piece // STRIP, strip)

    def slow_copy(k):
        return remote(fast.at[me, part(k)], slow_in.at[part(k)], slow_sem, k, partner)

    def gather_part(k):
        for j in range(1, chips):
            ag_copy(j, k, me).start()

    cast_slow(0)
    pl.semaphore_wait(barrier, chips + 1)

    def send_slow(k):
        slow_copy(k).start()

    send_slow(0)
    if early:
        gather_part(0)

    def cast_and_send(k):
        cast_slow(k)
        send_slow(k)

    def cast_and_gather(k):
        cast_and_send(k)
        gather_part(k)

    loop(early, cast_and_gather, start=1)
    loop(count, cast_and_send, start=max(early, 1))
    load(0).wait()
    load(1).wait()

    def make_grad(i):
        at = pl.ds(pl.multiple_of(i * STRIP, STRIP), STRIP)
        g, u = gate[at, :].astype(F32), ups[at, :].astype(F32)
        s = jax.nn.sigmoid(g)
        grad[at, :] = (u * g * s).astype(BF16)
        factor[at, :] = u * scale * s * (1.0 + g * (1.0 - s))

    loop(grad.shape[0] // STRIP, make_grad)

    load(2).wait()

    def first_hop(j, k):
        block = ahead(j) * 2 + 1 - core
        s1_out[j, part(k), :] = weight_part(block, k).astype(BF16)
        s1_copy(j, k).start()

    def second_hop(j, k):
        mine = weight_part(ahead(j) * 2 + core, k)
        s1_copy(j, k).wait_recv()
        s2_out[j - 1, part(k), :] = (mine + s1_in[j, part(k), :].astype(F32)).astype(BF16)
        s2_copy(j, k).start()

    remote_parts = (chips - 1) * count
    loop(remote_parts, lambda t: first_hop(lax.div(t, count) + 1, lax.rem(t, count)))
    loop(remote_parts, lambda t: second_hop(lax.div(t, count) + 1, lax.rem(t, count)))
    loop(count, lambda k: first_hop(0, k))
    loop(count, lambda k: fw_copy(0, k, me).start())

    def own_part(k):
        own[part(k), :] = weight_part(me, k)

    loop(count, own_part)

    def own_sum(k):
        s1_copy(0, k).wait_recv()
        for j in range(1, chips):
            s2_copy(j, k).wait_recv()

        def strip(i):
            at = pl.ds(pl.multiple_of(k * piece + i * STRIP, STRIP), STRIP)
            total = own[at, :] + s1_in[0, at, :].astype(F32)
            for j in range(1, chips):
                total = total + s2_in[j - 1, at, :].astype(F32)
            new = (inner_beta * imom[at, :].astype(F32) + total * scale).astype(BF16)
            inner_new[at, :] = new
            og = slow[at, :] - (fast[me, at, :].astype(F32) - inner_rate * new.astype(F32))
            own[at, :] = og
            og_out[at, :] = og.astype(BF16)

        loop(piece // STRIP, strip)
        og_copy(k).start()

    def up_part(block, k, first):
        start = pl.multiple_of(block * rows + k * piece, piece)
        value = jnp.dot(
            tok[:, pl.ds(start, piece)], fast[block, part(k), :], preferred_element_type=F32
        )
        acc[...] = value if first else acc[...] + value

    up_part(me, 0, True)
    loop(count, lambda k: up_part(me, k, False), start=1)

    def sibling_part(k):
        fw_copy(0, k, me).wait_recv()
        up_part(chip * 2 + 1 - core, k, False)

    loop(count, sibling_part)

    def gathered(j, k, last=False):
        block = behind(j) * 2 + core
        ag_copy(j, k, block).wait_recv()
        fw_copy(j, k, block).start()
        up_part(block, k, False)
        fw_copy(j, k, block).wait_recv()
        if not last:
            up_part(behind(j) * 2 + 1 - core, k, False)

    for j in range(1, chips):
        loop(early, functools.partial(gathered, j))
    load(3).wait()
    loop(count - 1, own_sum)
    loop(min(early + 1, count), gather_part, start=early)
    own_sum(count - 1)
    loop(count, gather_part, start=early + 1)

    def finish_weights():
        load(4).wait()

        def finish(k):
            slow_copy(k).wait_recv()
            og_copy(k).wait_recv()

            def strip(i):
                at = pl.ds(pl.multiple_of(k * piece + i * STRIP, STRIP), STRIP)
                mean_slow = 0.5 * (slow[at, :] + slow_in[at, :].astype(F32))
                mean_grad = 0.5 * (own[at, :] + og_in[at, :].astype(F32))
                new = (outer_mu * omom[at, :].astype(F32) + mean_grad).astype(BF16)
                outer_new[at, :] = new
                slow_new[at, :] = mean_slow - outer_rate * (
                    mean_grad + outer_mu * new.astype(F32)
                )

            loop(piece // STRIP, strip)

        loop(count, finish)

    def finish_gate():
        for j in range(1, chips - 1):
            loop(count, functools.partial(gathered, j), start=early)
        loop(count - 1, functools.partial(gathered, chips - 1), start=early)
        gathered(chips - 1, count - 1, last=True)
        block = behind(chips - 1) * 2 + 1 - core
        start = pl.multiple_of(block * rows + (count - 1) * piece, piece)

        def gate_piece(k):
            at = pl.ds(pl.multiple_of(k * tall, tall), tall)
            value = jnp.dot(
                tok[at, pl.ds(start, piece)], fast[block, part(count - 1), :],
                preferred_element_type=F32,
            )
            gate_grad[at, :] = ((acc[at, :] + value) * factor[at, :]).astype(BF16)

        loop(GATE_PIECES, gate_piece)

    if far:
        finish_gate()
        finish_weights()
    else:
        finish_weights()
        finish_gate()

    def drain(k):
        slow_copy(k).wait_send()
        og_copy(k).wait_send()
        for j in range(chips):
            s1_copy(j, k).wait_send()
            fw_copy(j, k, behind(j) * 2 + core).wait_send()
        for j in range(1, chips):
            s2_copy(j, k).wait_send()
            ag_copy(j, k, me).wait_send()

    loop(count, drain)


def outer_step(xor, n_rep, n, scale, tokens, gate_pre, upstream, slow, inner_mom, outer_mom):
    rows, cols = slow.shape
    held = tokens.shape[0]
    chips = n // 2
    count = rows // min(CHUNK, rows)
    hbm = pl.BlockSpec(memory_space=pl.ANY)
    flops = 4 * held * tokens.shape[1] * cols
    return pl.pallas_call(
        functools.partial(kernel, xor, n, 2 * xor >= n_rep, scale),
        out_shape=(
            pltpu.VMEM((held, cols), BF16),
            pltpu.VMEM((rows, cols), BF16),
            pltpu.VMEM((rows, cols), BF16),
            pltpu.VMEM((rows, cols), F32),
        ),
        in_specs=[hbm] * 6,
        out_specs=(pl.BlockSpec(memory_space=pltpu.VMEM),) * 4,
        scratch_shapes=[
            pltpu.VMEM(tokens.shape, BF16),
            pltpu.VMEM((held, cols), BF16),
            pltpu.VMEM((held, cols), BF16),
            pltpu.VMEM((rows, cols), F32),
            pltpu.VMEM((rows, cols), BF16),
            pltpu.VMEM((rows, cols), BF16),
            pltpu.VMEM((n, rows, cols), BF16),
            pltpu.VMEM((held, cols), BF16),
            pltpu.VMEM((chips, rows, cols), BF16),
            pltpu.VMEM((chips, rows, cols), BF16),
            pltpu.VMEM((chips - 1, rows, cols), BF16),
            pltpu.VMEM((chips - 1, rows, cols), BF16),
            pltpu.VMEM((rows, cols), F32),
            pltpu.VMEM((rows, cols), BF16),
            pltpu.VMEM((rows, cols), BF16),
            pltpu.VMEM((rows, cols), BF16),
            pltpu.VMEM((held, cols), F32),
            pltpu.VMEM((held, cols), F32),
            pltpu.SemaphoreType.DMA((5 + count,)),
            pltpu.SemaphoreType.DMA((2, count)),
            pltpu.SemaphoreType.DMA((2, chips * count)),
            pltpu.SemaphoreType.DMA((2, (chips - 1) * count)),
            pltpu.SemaphoreType.DMA((2, (chips - 1) * count)),
            pltpu.SemaphoreType.DMA((2, chips * count)),
            pltpu.SemaphoreType.DMA((2, count)),
        ],
        compiler_params=pltpu.CompilerParams(
            collective_id=xor, has_side_effects=True, vmem_limit_bytes=54 * 1024 * 1024
        ),
        cost_estimate=pl.CostEstimate(
            flops=flops, bytes_accessed=2 * tokens.size + 22 * slow.size, transcendentals=0
        ),
    )(tokens, gate_pre, upstream, slow, inner_mom, outer_mom)


def solution(mesh):
    n_rep, n = mesh.shape["rep"], mesh.shape["fsdp"]

    def local(tokens, gate_pre, upstream, slow, inner_mom, outer_mom, pairing):
        scale = float(tokens.shape[1]) ** -0.5
        branches = [
            functools.partial(outer_step, xor, n_rep, n, scale) for xor in range(1, n_rep)
        ]
        gate_grad, inner_new, outer_new, slow_new = lax.switch(
            pairing[0] - 1, branches,
            tokens, gate_pre, upstream, slow[0], inner_mom[0], outer_mom[0],
        )
        return gate_grad, inner_new[None], outer_new[None], slow_new[None]

    rows, weights = P(("rep", "fsdp"), None), P("rep", "fsdp", None)
    return jax.shard_map(
        local,
        mesh=mesh,
        in_specs=(rows, rows, rows, weights, weights, weights, P()),
        out_specs=(rows, weights, weights, weights),
        check_vma=False,
    )
```

```python
import functools

import jax
import jax.numpy as jnp
from jax import lax
from jax.experimental import pallas as pl
from jax.experimental.pallas import tpu as pltpu
from jax.sharding import PartitionSpec as P

inner_beta = 0.9
inner_rate = 0.5
outer_mu = 0.9
outer_rate = 0.7

MESH = pl.DeviceIdType.MESH
F32 = jnp.float32
BF16 = jnp.bfloat16
CHUNK = 256
STRIP = 16
GATE_PIECES = 4


def flipped(index, mask):
    out = index
    for bit in range(mask.bit_length()):
        if mask >> bit & 1:
            out = out + (1 - 2 * lax.rem(lax.div(index, 1 << bit), 2)) * (1 << bit)
    return out


def kernel(
    xor, n, far, scale,
    tok_hbm, gate_hbm, ups_hbm, slow_hbm, imom_hbm, omom_hbm,
    gate_grad, inner_new, outer_new, slow_new,
    tok, gate, ups, slow, imom, omom,
    fast, grad, s1_out, s1_in, s2_out, s2_in, own, og_out, og_in, slow_in, acc, factor,
    in_sem, slow_sem, s1_sem, s2_sem, ag_sem, fw_sem, og_sem,
):
    rows = slow.shape[0]
    piece = min(CHUNK, rows)
    count = rows // piece
    early = count // 2
    chips = n // 2
    rep, me = lax.axis_index("rep"), lax.axis_index("fsdp")
    chip, core = lax.div(me, 2), lax.rem(me, 2)
    sibling = (rep, chip * 2 + 1 - core)
    partner = (flipped(rep, xor), me)

    def ahead(j):
        return lax.rem(chip + j, chips)

    def behind(j):
        return lax.rem(chip + chips - j, chips)

    def part(k):
        return pl.ds(pl.multiple_of(k * piece, piece), piece)

    def weight_part(block, k):
        start = pl.multiple_of(block * rows + k * piece, piece)
        return lax.dot_general(
            tok[:, pl.ds(start, piece)], grad[...], (((0,), (0,)), ((), ())),
            preferred_element_type=F32,
        )

    def remote(src, dst, sems, slot, device):
        return pltpu.make_async_remote_copy(
            src_ref=src, dst_ref=dst, send_sem=sems.at[0, slot], recv_sem=sems.at[1, slot],
            device_id=device, device_id_type=MESH,
        )

    def s1_copy(j, k):
        return remote(s1_out.at[j, part(k)], s1_in.at[j, part(k)], s1_sem, j * count + k, sibling)

    def s2_copy(j, k):
        return remote(
            s2_out.at[j - 1, part(k)], s2_in.at[j - 1, part(k)], s2_sem, (j - 1) * count + k,
            (rep, ahead(j) * 2 + core),
        )

    def ag_copy(j, k, block):
        return remote(
            fast.at[block, part(k)], fast.at[block, part(k)], ag_sem, (j - 1) * count + k,
            (rep, ahead(j) * 2 + core),
        )

    def fw_copy(j, k, block):
        return remote(
            fast.at[block, part(k)], fast.at[block, part(k)], fw_sem, j * count + k, sibling
        )

    def og_copy(k):
        return remote(og_out.at[part(k)], og_in.at[part(k)], og_sem, k, partner)

    def loop(stop, body, start=0):
        def step(i, carry):
            body(i)
            return carry

        lax.fori_loop(start, stop, step, 0)

    def slow_load(k):
        return pltpu.make_async_copy(slow_hbm.at[part(k)], slow.at[part(k)], in_sem.at[5 + k])

    def load(i):
        src, dst = ((gate_hbm, gate), (ups_hbm, ups), (tok_hbm, tok), (imom_hbm, imom), (omom_hbm, omom))[i]
        return pltpu.make_async_copy(src, dst, in_sem.at[i])

    tall = gate_grad.shape[0] // GATE_PIECES

    barrier = pltpu.get_barrier_semaphore()
    pl.semaphore_signal(barrier, inc=1, device_id=sibling, device_id_type=MESH)
    pl.semaphore_signal(barrier, inc=1, device_id=partner, device_id_type=MESH)
    for j in range(1, chips):
        pl.semaphore_signal(
            barrier, inc=1, device_id=(rep, ahead(j) * 2 + core), device_id_type=MESH
        )

    slow_load(0).start()

    def cast_slow(k):
        slow_load(k).wait()

        def strip(i):
            at = pl.ds(pl.multiple_of(k * piece + i * STRIP, STRIP), STRIP)
            fast[me, at, :] = slow[at, :].astype(BF16)

        loop(piece // STRIP, strip)

    def slow_copy(k):
        return remote(fast.at[me, part(k)], slow_in.at[part(k)], slow_sem, k, partner)

    def gather_part(k):
        for j in range(1, chips):
            ag_copy(j, k, me).start()

    cast_slow(0)
    loop(count, lambda k: slow_load(k).start(), start=1)
    for i in range(5):
        load(i).start()
    pl.semaphore_wait(barrier, chips + 1)

    def send_slow(k):
        slow_copy(k).start()

    send_slow(0)
    if early:
        gather_part(0)

    def cast_and_send(k):
        cast_slow(k)
        send_slow(k)

    def cast_and_gather(k):
        cast_and_send(k)
        gather_part(k)

    loop(early, cast_and_gather, start=1)
    loop(count, cast_and_send, start=max(early, 1))
    load(0).wait()
    load(1).wait()

    def make_grad(i):
        at = pl.ds(pl.multiple_of(i * STRIP, STRIP), STRIP)
        g, u = gate[at, :].astype(F32), ups[at, :].astype(F32)
        s = jax.nn.sigmoid(g)
        grad[at, :] = (u * g * s).astype(BF16)
        factor[at, :] = u * scale * s * (1.0 + g * (1.0 - s))

    loop(grad.shape[0] // STRIP, make_grad)

    load(2).wait()

    def first_hop(j, k):
        block = ahead(j) * 2 + 1 - core
        s1_out[j, part(k), :] = weight_part(block, k).astype(BF16)
        s1_copy(j, k).start()

    def second_hop(j, k):
        mine = weight_part(ahead(j) * 2 + core, k)
        s1_copy(j, k).wait_recv()
        s2_out[j - 1, part(k), :] = (mine + s1_in[j, part(k), :].astype(F32)).astype(BF16)
        s2_copy(j, k).start()

    remote_parts = (chips - 1) * count
    loop(remote_parts, lambda t: first_hop(lax.div(t, count) + 1, lax.rem(t, count)))
    loop(remote_parts, lambda t: second_hop(lax.div(t, count) + 1, lax.rem(t, count)))
    loop(count, lambda k: first_hop(0, k))
    loop(count, lambda k: fw_copy(0, k, me).start())

    def own_part(k):
        own[part(k), :] = weight_part(me, k)

    loop(count, own_part)

    def own_sum(k):
        s1_copy(0, k).wait_recv()
        for j in range(1, chips):
            s2_copy(j, k).wait_recv()

        def strip(i):
            at = pl.ds(pl.multiple_of(k * piece + i * STRIP, STRIP), STRIP)
            total = own[at, :] + s1_in[0, at, :].astype(F32)
            for j in range(1, chips):
                total = total + s2_in[j - 1, at, :].astype(F32)
            new = (inner_beta * imom[at, :].astype(F32) + total * scale).astype(BF16)
            inner_new[at, :] = new
            og = slow[at, :] - (fast[me, at, :].astype(F32) - inner_rate * new.astype(F32))
            own[at, :] = og
            og_out[at, :] = og.astype(BF16)

        loop(piece // STRIP, strip)
        og_copy(k).start()

    def up_part(block, k, first):
        start = pl.multiple_of(block * rows + k * piece, piece)
        value = jnp.dot(
            tok[:, pl.ds(start, piece)], fast[block, part(k), :], preferred_element_type=F32
        )
        acc[...] = value if first else acc[...] + value

    up_part(me, 0, True)
    loop(count, lambda k: up_part(me, k, False), start=1)

    def sibling_part(k):
        fw_copy(0, k, me).wait_recv()
        up_part(chip * 2 + 1 - core, k, False)

    loop(count, sibling_part)

    def gathered(j, k, last=False):
        block = behind(j) * 2 + core
        ag_copy(j, k, block).wait_recv()
        fw_copy(j, k, block).start()
        up_part(block, k, False)
        fw_copy(j, k, block).wait_recv()
        if not last:
            up_part(behind(j) * 2 + 1 - core, k, False)

    for j in range(1, chips):
        loop(early, functools.partial(gathered, j))
    load(3).wait()
    loop(count - 1, own_sum)
    loop(min(early + 1, count), gather_part, start=early)
    own_sum(count - 1)
    loop(count, gather_part, start=early + 1)

    def finish_weights():
        load(4).wait()

        def finish(k):
            slow_copy(k).wait_recv()
            og_copy(k).wait_recv()

            def strip(i):
                at = pl.ds(pl.multiple_of(k * piece + i * STRIP, STRIP), STRIP)
                mean_slow = 0.5 * (slow[at, :] + slow_in[at, :].astype(F32))
                mean_grad = 0.5 * (own[at, :] + og_in[at, :].astype(F32))
                new = (outer_mu * omom[at, :].astype(F32) + mean_grad).astype(BF16)
                outer_new[at, :] = new
                slow_new[at, :] = mean_slow - outer_rate * (
                    mean_grad + outer_mu * new.astype(F32)
                )

            loop(piece // STRIP, strip)

        loop(count, finish)

    def finish_gate():
        for j in range(1, chips - 1):
            loop(count, functools.partial(gathered, j), start=early)
        loop(count - 1, functools.partial(gathered, chips - 1), start=early)
        gathered(chips - 1, count - 1, last=True)
        block = behind(chips - 1) * 2 + 1 - core
        start = pl.multiple_of(block * rows + (count - 1) * piece, piece)

        def gate_piece(k):
            at = pl.ds(pl.multiple_of(k * tall, tall), tall)
            value = jnp.dot(
                tok[at, pl.ds(start, piece)], fast[block, part(count - 1), :],
                preferred_element_type=F32,
            )
            gate_grad[at, :] = ((acc[at, :] + value) * factor[at, :]).astype(BF16)

        loop(GATE_PIECES, gate_piece)

    if far:
        finish_gate()
        finish_weights()
    else:
        finish_weights()
        finish_gate()

    def drain(k):
        slow_copy(k).wait_send()
        og_copy(k).wait_send()
        for j in range(chips):
            s1_copy(j, k).wait_send()
            fw_copy(j, k, behind(j) * 2 + core).wait_send()
        for j in range(1, chips):
            s2_copy(j, k).wait_send()
            ag_copy(j, k, me).wait_send()

    loop(count, drain)


def outer_step(xor, n_rep, n, scale, tokens, gate_pre, upstream, slow, inner_mom, outer_mom):
    rows, cols = slow.shape
    held = tokens.shape[0]
    chips = n // 2
    count = rows // min(CHUNK, rows)
    hbm = pl.BlockSpec(memory_space=pl.ANY)
    flops = 4 * held * tokens.shape[1] * cols
    return pl.pallas_call(
        functools.partial(kernel, xor, n, 2 * xor >= n_rep, scale),
        out_shape=(
            pltpu.VMEM((held, cols), BF16),
            pltpu.VMEM((rows, cols), BF16),
            pltpu.VMEM((rows, cols), BF16),
            pltpu.VMEM((rows, cols), F32),
        ),
        in_specs=[hbm] * 6,
        out_specs=(pl.BlockSpec(memory_space=pltpu.VMEM),) * 4,
        scratch_shapes=[
            pltpu.VMEM(tokens.shape, BF16),
            pltpu.VMEM((held, cols), BF16),
            pltpu.VMEM((held, cols), BF16),
            pltpu.VMEM((rows, cols), F32),
            pltpu.VMEM((rows, cols), BF16),
            pltpu.VMEM((rows, cols), BF16),
            pltpu.VMEM((n, rows, cols), BF16),
            pltpu.VMEM((held, cols), BF16),
            pltpu.VMEM((chips, rows, cols), BF16),
            pltpu.VMEM((chips, rows, cols), BF16),
            pltpu.VMEM((chips - 1, rows, cols), BF16),
            pltpu.VMEM((chips - 1, rows, cols), BF16),
            pltpu.VMEM((rows, cols), F32),
            pltpu.VMEM((rows, cols), BF16),
            pltpu.VMEM((rows, cols), BF16),
            pltpu.VMEM((rows, cols), BF16),
            pltpu.VMEM((held, cols), F32),
            pltpu.VMEM((held, cols), F32),
            pltpu.SemaphoreType.DMA((5 + count,)),
            pltpu.SemaphoreType.DMA((2, count)),
            pltpu.SemaphoreType.DMA((2, chips * count)),
            pltpu.SemaphoreType.DMA((2, (chips - 1) * count)),
            pltpu.SemaphoreType.DMA((2, (chips - 1) * count)),
            pltpu.SemaphoreType.DMA((2, chips * count)),
            pltpu.SemaphoreType.DMA((2, count)),
        ],
        compiler_params=pltpu.CompilerParams(
            collective_id=xor, has_side_effects=True, vmem_limit_bytes=54 * 1024 * 1024
        ),
        cost_estimate=pl.CostEstimate(
            flops=flops, bytes_accessed=2 * tokens.size + 22 * slow.size, transcendentals=0
        ),
    )(tokens, gate_pre, upstream, slow, inner_mom, outer_mom)


def solution(mesh):
    n_rep, n = mesh.shape["rep"], mesh.shape["fsdp"]

    def local(tokens, gate_pre, upstream, slow, inner_mom, outer_mom, pairing):
        scale = float(tokens.shape[1]) ** -0.5
        branches = [
            functools.partial(outer_step, xor, n_rep, n, scale) for xor in range(1, n_rep)
        ]
        gate_grad, inner_new, outer_new, slow_new = lax.switch(
            pairing[0] - 1, branches,
            tokens, gate_pre, upstream, slow[0], inner_mom[0], outer_mom[0],
        )
        return gate_grad, inner_new[None], outer_new[None], slow_new[None]

    rows, weights = P(("rep", "fsdp"), None), P("rep", "fsdp", None)
    return jax.shard_map(
        local,
        mesh=mesh,
        in_specs=(rows, rows, rows, weights, weights, weights, P()),
        out_specs=(rows, weights, weights, weights),
        check_vma=False,
    )
```
